256 devices in a mesh: ctx: 16 (over x, z_lo, core), head: 16 (over z_hi, y).
Axes of the slice: x: 4, y: 4, z: 8 (z_hi: 4, z_lo: 2; z = z_hi * 2 + z_lo), core: 2. Of those that a mesh axis runs over, the one named last changes fastest.
Arguments:
- queries: bfloat16 [16384, 8192], P(('ctx', 'head')), may hold values from -13.5 to 13.5
- span_keys: bfloat16 [16384, 1024], P(('ctx', 'head')), may hold values from -13.5 to 13.5
- span_values: bfloat16 [16384, 1024], P(('ctx', 'head')), may hold values from -4 to 4
- cache_keys: bfloat16 [16384, 1024], P('ctx'), may hold values from -4 to 4
- cache_values: bfloat16 [16384, 1024], P('ctx'), may hold values from -4 to 4
- verticals: int32 [64, 16, 1], P('head'), may hold values from 0 to 15
- slashes: int32 [64, 3], P('head'), may hold values from 1 to 255
Outputs:
- attended: bfloat16 [16384, 8192], P(('ctx', 'head'))
The draws below stay inside these ranges and needn't reach their ends.
All inputs are finite; a program needn't handle non-finite values.
Results may differ from the reference program's by a relative error of at most 0.009.
Values may be sent and summed in bfloat16 or wider, within the bound.
No kernel may reach another device: no remote copies, remote signals or barrier semaphores. Data moves between devices by JAX's collectives and lax.ppermute only.
A program may use at most 128 MiB of HBM per device.

```python
import jax
import jax.numpy as jnp
from jax import lax

H = 64
KVH = 8
DH = 128
BLK = 128
NV = 1
NS = 3
CACHE_DEV = 1024
SLAB = 1024
SPAN = 16384
CACHE = 16384
SHARD_BLOCKS = 16
ALL_BLOCKS = 256
N_CTX = 16


def draw_queries(key, part):
    key = jax.random.fold_in(key, 1)
    values = jnp.clip(jax.random.normal(key, (SPAN, H, DH), jnp.float32), -4.0, 4.0)
    return values.reshape(SPAN, H * DH).astype(jnp.bfloat16)


def draw_span_keys(key, part):
    key = jax.random.fold_in(key, 2)
    values = jnp.clip(jax.random.normal(key, (SPAN, KVH, DH), jnp.float32), -4.0, 4.0)
    return values.reshape(SPAN, KVH * DH).astype(jnp.bfloat16)


def set_ends(values, rng, low, high):
    index_at = [jax.random.randint(jax.random.fold_in(rng, axis), (), 0, length) for axis, length in enumerate(values.shape)]
    longest = values.shape.index(max(values.shape))
    neighbour = index_at[:longest] + [(index_at[longest] + 1) % values.shape[longest]] + index_at[longest + 1:]
    return values.at[tuple(index_at)].set(low).at[tuple(neighbour)].set(high)


def block_scale(own_key, dims, split, low, top_value):
    factor_of, own = 1.0, jax.random.fold_in(own_key, 6)
    for dim, parts in split:
        heights = jnp.exp(jax.random.uniform(jax.random.fold_in(own, dim), (parts,), jnp.float32, low / len(split), top_value / len(split)))
        factor_of = factor_of * jnp.repeat(heights, dims[dim] // parts).reshape([-1 if axis == dim else 1 for axis in range(len(dims))])
    return factor_of


def bell_draw(own_key, dims, deviation, limit, cuts=(), kind=jnp.bfloat16):
    values = deviation * jax.random.normal(own_key, dims, jnp.float32)
    if cuts:
        values = values * block_scale(own_key, dims, cuts, -0.22, 0.18)
    return jnp.clip(values, -limit, limit).astype(kind)


def setup_inputs(seed: int = 0) -> dict:
    key_list = jax.random.split(jax.random.key(seed), 8)
    queries = draw_queries(jax.random.fold_in(key_list[7], 71), 0)
    span_keys = draw_span_keys(jax.random.fold_in(key_list[7], 71), 0)
    span_values = bell_draw(key_list[2], (SPAN, KVH * DH), 1.0, 4.0, ((0, 256),))
    cache_keys = bell_draw(key_list[3], (CACHE, KVH * DH), 1.0, 4.0, ((0, 16),))
    cache_values = bell_draw(key_list[4], (CACHE, KVH * DH), 1.0, 4.0, ((0, 16),))
    verticals = set_ends(jax.random.randint(key_list[5], (H, N_CTX, NV), 0, SHARD_BLOCKS), jax.random.fold_in(key_list[5], 1), 0, SHARD_BLOCKS - 1).astype(jnp.int32)
    slashes = set_ends(jax.random.randint(key_list[6], (H, NS), 1, ALL_BLOCKS), jax.random.fold_in(key_list[6], 1), 1, ALL_BLOCKS - 1).astype(jnp.int32)
    return {"queries": queries, "span_keys": span_keys, "span_values": span_values, "cache_keys": cache_keys, "cache_values": cache_values, "verticals": verticals, "slashes": slashes}


masked_score = -1.0e30


def reference(queries, span_keys, span_values, cache_keys, cache_values, verticals, slashes):
    group_size = H // KVH
    shard_cache = CACHE_DEV // BLK
    shard_span = SLAB // BLK
    cache_blocks = CACHE // BLK
    query_count = SPAN // BLK
    total_blocks = (CACHE + SPAN) // BLK
    keys_all = jnp.concatenate([cache_keys, span_keys], axis=0).reshape(total_blocks, BLK, KVH, DH).transpose(2, 0, 1, 3)
    values_all = jnp.concatenate([cache_values, span_values], axis=0).reshape(total_blocks, BLK, KVH, DH).transpose(2, 0, 1, 3)
    heads_q = queries.reshape(query_count, BLK, H, DH).transpose(2, 0, 1, 3)
    shard_ids = jnp.arange(N_CTX, dtype=jnp.int32)[:, None]
    query_blocks = cache_blocks + jnp.arange(query_count, dtype=jnp.int32)
    offset_list = jnp.concatenate([jnp.zeros((H, 1), jnp.int32), slashes.astype(jnp.int32)], axis=1)
    inside_range = jnp.arange(BLK, dtype=jnp.int32)

    def one_head(element):
        head_index, query_head_rows, vertical, offsets = element
        kv_head = head_index // group_size
        key_rows = keys_all[kv_head]
        value_rows = values_all[kv_head]
        vertical_abs = jnp.where(vertical < shard_cache, shard_ids * shard_cache + vertical,
                                 cache_blocks + shard_ids * shard_span + vertical - shard_cache).reshape(-1)
        targets = query_blocks[:, None] - offsets[None, :]
        absolute = jnp.concatenate([jnp.broadcast_to(vertical_abs[None, :], (query_count, vertical_abs.shape[0])), targets], axis=1)
        usable = jnp.concatenate([jnp.ones((query_count, vertical_abs.shape[0]), bool), targets >= 0], axis=1)
        position = jnp.arange(absolute.shape[1], dtype=jnp.int32)
        earlier = position[None, :] < position[:, None]
        repeated = (absolute[:, :, None] == absolute[:, None, :]) & usable[:, None, :] & earlier[None]
        usable = usable & jnp.logical_not(jnp.any(repeated, axis=-1))
        picked = jnp.maximum(absolute, 0)
        selected_key_blocks = jnp.take(key_rows, picked, axis=0).astype(jnp.float32)
        selected_value_blocks = jnp.take(value_rows, picked, axis=0).astype(jnp.float32)
        key_pos = picked[:, :, None] * BLK + inside_range
        query_pos = query_blocks[:, None] * BLK + inside_range
        allowed = usable[:, None, :, None] & (key_pos[:, None, :, :] <= query_pos[:, :, None, None])
        logit_matrix = jnp.einsum("vot,vgyt->vogy", query_head_rows.astype(jnp.float32), selected_key_blocks,
                            precision=lax.Precision.HIGHEST) * (DH ** -0.5)
        logit_matrix = jnp.where(allowed, logit_matrix, masked_score)
        row_max = jnp.max(logit_matrix, axis=(2, 3))
        weights = jnp.where(allowed, jnp.exp(logit_matrix - row_max[:, :, None, None]), 0.0)
        lowered_precision = lax.optimization_barrier(weights.astype(jnp.bfloat16)).astype(jnp.float32)
        weighted_output = jnp.einsum("hufr,hfro->huo", lowered_precision, selected_value_blocks, precision=lax.Precision.HIGHEST)
        return (weighted_output / jnp.sum(weights, axis=(2, 3))[:, :, None]).astype(jnp.bfloat16)

    outputs = lax.map(one_head, (jnp.arange(H, dtype=jnp.int32), heads_q, verticals.astype(jnp.int32), offset_list))
    return outputs.transpose(1, 2, 0, 3).reshape(SPAN, H * DH)
```

```python
import functools

import jax
import jax.numpy as jnp
import numpy as np
from jax import lax
from jax.experimental import pallas as pl
from jax.experimental.pallas import tpu as pltpu
from jax.sharding import Mesh
from jax.sharding import PartitionSpec as P

H = 64
KVH = 8
DH = 128
BLK = 128
GROUP = H // KVH
HALF = 64
NLIST = 20
GRP = 4
masked_score = -1e30
SCALE = DH ** (-0.5) * 1.4426950408889634


def shift(value, axis, size, step):
    return lax.ppermute(value, axis, [(i, (i + step) % size) for i in range(size)])


def ring_direct(value, axis):
    return [value, shift(value, axis, 4, 1), shift(value, axis, 4, -1), shift(value, axis, 4, 2)]


ORIGINS = (0, -1, 1, 2)
PLANES = (0, 2, 4, 6, 1, 3, 5, 7)


HBM = pl.BlockSpec(memory_space=pl.ANY)
SMEM = pl.BlockSpec(memory_space=pltpu.SMEM)
VMEM = pl.BlockSpec(memory_space=pltpu.VMEM)


def shaped(shape, dtype=jnp.bfloat16):
    return jax.ShapeDtypeStruct(shape, dtype)


def payload_kernel(place, cache_keys, cache_values, span_keys, span_values, own, other, span, sems):
    start = pl.multiple_of(place[1] * 256, 256)
    plane, near = place[3], place[4]
    copies = []
    for i, cache in enumerate((cache_keys, cache_values)):
        for j, (target, column) in enumerate(((own, plane), (other, near))):
            lanes = pl.ds(pl.multiple_of(column * DH, DH), DH)
            copies.append(
                pltpu.make_async_copy(cache.at[pl.ds(start, 256), lanes], target.at[i], sems.at[2 * i + j])
            )
    for copy in copies:
        copy.start()
    for i, source in enumerate((span_keys, span_values)):
        for slot, p in enumerate(PLANES):
            span[slot, i] = source[:, p * DH : (p + 1) * DH]
    for copy in copies:
        copy.wait()


def payload(place, cache_keys, cache_values, span_keys, span_values):
    return pl.pallas_call(
        payload_kernel,
        out_shape=[shaped((2, 256, DH)), shaped((2, 256, DH)), shaped((8, 2, HALF, DH))],
        in_specs=[SMEM, HBM, HBM, VMEM, VMEM],
        out_specs=[VMEM, VMEM, VMEM],
        scratch_shapes=[pltpu.SemaphoreType.DMA((4,))],
        name="payload",
    )(place, cache_keys, cache_values, span_keys, span_values)


def merge_kernel(extra, place, own, swapped, *refs):
    zl = place[5]
    for i, target in enumerate(refs[extra:]):
        target[zl] = own[i]
        target[1 - zl] = swapped[i]


def merge(place, own, swapped, after=()):
    return pl.pallas_call(
        functools.partial(merge_kernel, len(after)),
        out_shape=[shaped((2, 256, DH))] * 2,
        in_specs=[SMEM, VMEM, VMEM] + [HBM] * len(after),
        out_specs=[VMEM, VMEM],
        name="merge",
    )(place, own, swapped, *after)


def stack_kernel(*refs):
    for i, source in enumerate(refs[:8]):
        refs[8 + i // 4][i % 4] = source[...]


def stack(keys, values):
    shape = (4,) + keys[0].shape
    return pl.pallas_call(
        stack_kernel,
        out_shape=[shaped(shape)] * 2,
        in_specs=[VMEM] * 8,
        out_specs=[VMEM, VMEM],
        name="stack",
    )(*keys, *values)


def plane_kernel(extra, source, *refs):
    target = refs[extra]
    width = GROUP * DH
    for slot, plane in enumerate(PLANES):
        target[slot] = source[:, plane * width : (plane + 1) * width]


def by_plane(queries, after=()):
    return pl.pallas_call(
        functools.partial(plane_kernel, len(after)),
        out_shape=shaped((8, HALF, GROUP * DH)),
        in_specs=[VMEM] + [HBM] * len(after),
        out_specs=VMEM,
        name="by_plane",
    )(queries, *after)


def second_stage(plan, arrays, slots, is_value):
    x_first = not is_value
    pieces = ring_direct(slots, "y" if x_first else "x")
    for array, origin in zip(pieces, ORIGINS):
        for other in range(2):
            plan.append((is_value, x_first, origin, other))
            arrays.append((shift(array, "k", 2, 1) if other else array).reshape(4, 2, 2, BLK, DH))
    return pieces


def attention_kernel(plan, place, picks, biases, q_ref, span_ref, *refs):
    pieces = refs[: len(plan)]
    out_ref, kbuf, vbuf, sems = refs[len(plan) :]
    my_x, my_y, my_k = place[0], place[1], place[2]
    copies = []

    def copy(source, target):
        copies.append(pltpu.make_async_copy(source, target, sems.at[len(copies)]))

    for piece, (is_value, x_first, origin, other) in zip(pieces, plan):
        buffer = vbuf if is_value else kbuf
        for slot, near in enumerate(ORIGINS):
            dx, dy = (near, origin) if x_first else (origin, near)
            from_x = lax.rem(my_x + (dx + 4), 4)
            from_y = lax.rem(my_y + (dy + 4), 4)
            from_k = 1 - my_k if other else my_k
            copy(piece.at[slot], buffer.at[0, from_x, :, from_k, from_y])
    for x in range(4):
        for k in range(2):
            for y in range(4):
                slot = (x * 2 + k) * 4 + y
                for is_value, buffer in enumerate((kbuf, vbuf)):
                    copy(
                        span_ref.at[pl.ds(2 * slot, 2), :, is_value],
                        buffer.at[1, x, :, k, :, y // 2, pl.ds(y % 2 * HALF, HALF), :],
                    )
    for entry in copies:
        entry.start()
    for entry in copies:
        entry.wait()

    keys = kbuf.reshape(256, BLK, DH)
    values = vbuf.reshape(256, BLK, DH)
    half = lax.rem(my_y, 2) * HALF
    rows = lax.broadcasted_iota(jnp.int32, (HALF, BLK), 0) + half
    cols = lax.broadcasted_iota(jnp.int32, (HALF, BLK), 1)
    triangle = cols <= rows
    dims = (((1,), (1,)), ((), ()))

    def step(item, carry):
        head = lax.div(item, 8 // GRP)
        part = lax.rem(item, 8 // GRP)
        lane = pl.ds(pl.multiple_of(head * DH, DH), DH)
        base = [(head * 8 + part * GRP + r) * NLIST for r in range(GRP)]
        q = [q_ref[part * GRP + r, :, lane] for r in range(GRP)]
        q_all = jnp.concatenate(q, axis=0)
        scores = [[] for _ in range(GRP)]

        def pick(ref, start, e):
            return jnp.concatenate([ref[picks[start + e]], ref[picks[start + e + 1]]], axis=0)

        def put(r, e, s):
            for d in range(2):
                block = s[:, d * BLK : (d + 1) * BLK]
                if e + d == 0:
                    block = jnp.where(triangle, block, masked_score)
                else:
                    block = block + biases[base[r] + e + d]
                scores[r].append(block)

        for e in range(0, 4, 2):
            for r in range(GRP):
                s = lax.dot_general(q[r], pick(keys, base[r], e), dims, preferred_element_type=jnp.float32)
                put(r, e, s)
        for e in range(4, NLIST, 2):
            s = lax.dot_general(q_all, pick(keys, base[0], e), dims, preferred_element_type=jnp.float32)
            for r in range(GRP):
                put(r, e, s[r * HALF : (r + 1) * HALF])
        weights = []
        inverse = []
        for r in range(GRP):
            top = functools.reduce(jnp.maximum, scores[r])
            top = jnp.max(top, axis=1, keepdims=True) * SCALE
            w = [jnp.exp2(s * SCALE - top) for s in scores[r]]
            total = jnp.sum(functools.reduce(jnp.add, w), axis=1, keepdims=True)
            inverse.append(1.0 / total)
            weights.append([a.astype(jnp.bfloat16) for a in w])
        summed = []
        for r in range(GRP):
            acc = jnp.zeros((HALF, DH), jnp.float32)
            for e in range(0, 4, 2):
                pair = jnp.concatenate(weights[r][e : e + 2], axis=1)
                acc = acc + jnp.dot(pair, pick(values, base[r], e), preferred_element_type=jnp.float32)
            summed.append(acc)
        acc = jnp.concatenate(summed, axis=0)
        for e in range(4, NLIST, 2):
            pair = jnp.concatenate(
                [jnp.concatenate(weights[r][e : e + 2], axis=1) for r in range(GRP)], axis=0
            )
            acc = acc + jnp.dot(pair, pick(values, base[0], e), preferred_element_type=jnp.float32)
        for r in range(GRP):
            result = acc[r * HALF : (r + 1) * HALF] * inverse[r]
            out_ref[part * GRP + r, :, lane] = result.astype(jnp.bfloat16)
        return carry

    lax.fori_loop(0, GROUP * 8 // GRP, step, 0)


def head_table(table, my_y, zl):
    around = jnp.stack(ring_direct(table, "y"))
    origins = (my_y + jnp.array([0, 3, 1, 2], jnp.int32)) % 4

    def of(wanted):
        return jnp.sum(jnp.where((origins == wanted)[:, None, None], around, 0), axis=0)

    return jnp.concatenate([of(2 * zl), of(2 * zl + 1)], axis=0)


def listed_blocks(table, my_x, my_y, my_k):
    verticals, slashes = table[:, :16], table[:, 16:]
    shard = jnp.arange(16, dtype=jnp.int32)
    vertical = shard * 8 + verticals + jnp.where(verticals >= 8, 120, 0)
    zl = jnp.arange(8, dtype=jnp.int32) // 4
    zh = jnp.arange(8, dtype=jnp.int32) % 4
    own = 128 + (my_x * 4 + zl * 2 + my_k) * 8 + zh * 2 + my_y // 2
    target = own[None, :, None] - slashes[:, None, :]
    before = jnp.arange(3)[None, :] < jnp.arange(3)[:, None]
    repeated = jnp.any((slashes[:, :, None] == slashes[:, None, :]) & before, axis=-1)
    listed = jnp.any(target[..., None] == vertical[:, None, None, :], axis=-1)
    slash_ok = (target >= 0) & jnp.logical_not(repeated[:, None, :]) & jnp.logical_not(listed)
    vertical_ok = vertical[:, None, :] < own[None, :, None]
    shape = (GROUP, 8, 1)
    picks = jnp.concatenate(
        [
            jnp.broadcast_to(own[None, :, None], shape),
            jnp.maximum(target, 0),
            jnp.broadcast_to(vertical[:, None, :], (GROUP, 8, 16)),
        ],
        axis=2,
    )
    usable = jnp.concatenate([jnp.ones(shape, bool), slash_ok, vertical_ok], axis=2)
    biases = jnp.where(usable, 0.0, masked_score).astype(jnp.float32)
    return picks.reshape(-1), biases.reshape(-1)


def per_device(queries, span_keys, span_values, cache_keys, cache_values, verticals, slashes):
    my_x, my_y, my_k = lax.axis_index("x"), lax.axis_index("y"), lax.axis_index("k")
    zh, zl = lax.axis_index("zh"), lax.axis_index("zl")
    plane = zh * 2 + zl
    zaxes = ("zl", "zh")

    table = jnp.concatenate([verticals[:, :, 0], slashes], axis=1)
    table = head_table(table, my_y, zl)

    place = jnp.stack([my_x, my_y, my_k, plane, plane + 1 - 2 * zl, zl]).astype(jnp.int32)
    own, other, span = payload(place, cache_keys, cache_values, span_keys, span_values)
    swapped = shift(other, "zl", 2, 1)
    span = lax.all_to_all(span, zaxes, split_axis=0, concat_axis=0, tiled=True)

    span = lax.all_gather(span, ("x", "k", "y"), axis=0, tiled=True)
    span = span.reshape(64, 4, 2, HALF, DH)

    plan = []
    arrays = []
    cache_k, cache_v = merge(place, own, swapped, (table,))
    cache_k, cache_v = stack(ring_direct(cache_k, "x"), ring_direct(cache_v, "y"))
    second_stage(plan, arrays, cache_k, False)
    second_stage(plan, arrays, cache_v, True)
    slab_queries = lax.all_to_all(
        by_plane(queries, (cache_k,)), zaxes, split_axis=0, concat_axis=0, tiled=True
    )

    picks, biases = listed_blocks(table, my_x, my_y, my_k)
    buffer = (2, 4, 2, 2, 4, 2, BLK, DH)
    attended = pl.pallas_call(
        functools.partial(attention_kernel, tuple(plan)),
        out_shape=jax.ShapeDtypeStruct((8, HALF, GROUP * DH), jnp.bfloat16),
        in_specs=[SMEM, SMEM, SMEM, VMEM] + [HBM] * (1 + len(arrays)),
        out_specs=VMEM,
        scratch_shapes=[
            pltpu.VMEM(buffer, jnp.bfloat16),
            pltpu.VMEM(buffer, jnp.bfloat16),
            pltpu.SemaphoreType.DMA((4 * len(arrays) + 64,)),
        ],
        compiler_params=pltpu.CompilerParams(vmem_limit_bytes=50 * 1024 * 1024),
        cost_estimate=pl.CostEstimate(
            flops=2 * 2 * 64 * 64 * 2560 * 128, bytes_accessed=18 << 20, transcendentals=10 << 20
        ),
        name="attention",
    )(place, picks, biases, slab_queries, span, *arrays)
    result = lax.all_to_all(attended, zaxes, split_axis=0, concat_axis=0, tiled=True)
    return jnp.concatenate([result[PLANES.index(p)] for p in range(8)], axis=1)


def solution(mesh):
    axes = ("x", "zl", "k", "zh", "y")
    fine = Mesh(np.asarray(mesh.devices).reshape(4, 2, 2, 4, 4), axes)
    rows = P(axes, None)
    return jax.shard_map(
        per_device,
        mesh=fine,
        in_specs=(
            rows,
            rows,
            rows,
            P(("x", "zl", "k"), None),
            P(("x", "zl", "k"), None),
            P(("zh", "y"), None, None),
            P(("zh", "y"), None),
        ),
        out_specs=rows,
        check_vma=False,
    )
```

```python
import functools

import jax
import jax.numpy as jnp
import numpy as np
from jax import lax
from jax.experimental import pallas as pl
from jax.experimental.pallas import tpu as pltpu
from jax.sharding import Mesh
from jax.sharding import PartitionSpec as P

H = 64
KVH = 8
DH = 128
BLK = 128
GROUP = H // KVH
HALF = 64
NLIST = 20
LARGEST = 2.0**90
masked_score = -1e30
SCALE = DH ** (-0.5) * 1.4426950408889634


def shift(value, axis, size, step):
    return lax.ppermute(value, axis, [(i, (i + step) % size) for i in range(size)])


def ring_direct(value, axis):
    return [value, shift(value, axis, 4, 1), shift(value, axis, 4, -1), shift(value, axis, 4, 2)]


ORIGINS = (0, -1, 1, 2)
PLANES = (0, 2, 4, 6, 1, 3, 5, 7)


HBM = pl.BlockSpec(memory_space=pltpu.HBM)
SMEM = pl.BlockSpec(memory_space=pltpu.SMEM)
VMEM = pl.BlockSpec(memory_space=pltpu.VMEM)


def shaped(shape, dtype=jnp.bfloat16):
    return jax.ShapeDtypeStruct(shape, dtype)


def payload_kernel(place, cache_keys, cache_values, span_keys, span_values, own, other, span, sems):
    start = pl.multiple_of(place[1] * 256, 256)
    copies = []
    for i, cache in enumerate((cache_keys, cache_values)):
        for j, (target, column) in enumerate(((own, place[3]), (other, place[4]))):
            lanes = pl.ds(pl.multiple_of(column * DH, DH), DH)
            copies.append(
                pltpu.make_async_copy(cache.at[pl.ds(start, 256), lanes], target.at[i], sems.at[2 * i + j])
            )
    for copy in copies:
        copy.start()
    for i, source in enumerate((span_keys, span_values)):
        for slot, p in enumerate(PLANES):
            span[slot, i] = source[:, p * DH : (p + 1) * DH]
    for copy in copies:
        copy.wait()


def payload(place, cache_keys, cache_values, span_keys, span_values):
    return pl.pallas_call(
        payload_kernel,
        out_shape=[shaped((2, 256, DH)), shaped((2, 256, DH)), shaped((8, 2, HALF, DH))],
        in_specs=[SMEM, HBM, HBM, VMEM, VMEM],
        out_specs=[VMEM, VMEM, VMEM],
        scratch_shapes=[pltpu.SemaphoreType.DMA((4,))],
        compiler_params=pltpu.CompilerParams(vmem_limit_bytes=56 * 1024 * 1024),
        name="payload",
    )(place, cache_keys, cache_values, span_keys, span_values)


def pack_kernel(own, swapped, span, out):
    for i in range(2):
        out[0, i] = own[i]
        out[1, i] = swapped[i]
        for zl in range(2):
            for zh in range(4):
                out[2 + zl, i, zh * HALF : (zh + 1) * HALF] = span[zl * 4 + zh, i]


def pack(own, swapped, span):
    return pl.pallas_call(
        pack_kernel,
        out_shape=shaped((4, 2, 256, DH)),
        in_specs=[VMEM] * 3,
        out_specs=VMEM,
        name="pack",
    )(own, swapped, span)


def plane_kernel(extra, source, *refs):
    target = refs[extra]
    width = GROUP * DH
    for slot, plane in enumerate(PLANES):
        target[slot] = source[:, plane * width : (plane + 1) * width]


def by_plane(queries, after=()):
    return pl.pallas_call(
        functools.partial(plane_kernel, len(after)),
        out_shape=shaped((8, HALF, GROUP * DH)),
        in_specs=[VMEM] + [HBM] * len(after),
        out_specs=VMEM,
        name="by_plane",
    )(queries, *after)


BUFFER = (2, 4, 2, 2, 4, 2, BLK, DH)


def attend(exact, place, picks, biases, q_ref, keys, values, out_ref):
    group = 4 if exact else 8
    half = lax.rem(place[1], 2) * HALF
    rows = lax.broadcasted_iota(jnp.int32, (HALF, BLK), 0) + half
    cols = lax.broadcasted_iota(jnp.int32, (HALF, BLK), 1)
    triangle = cols <= rows
    dims = (((1,), (1,)), ((), ()))

    def step(item, largest):
        head = lax.div(item, 8 // group)
        part = lax.rem(item, 8 // group)
        lane = pl.ds(pl.multiple_of(head * DH, DH), DH)
        base = [(head * 8 + part * group + r) * NLIST for r in range(group)]
        q = [q_ref[part * group + r, :, lane] for r in range(group)]
        q_all = jnp.concatenate(q, axis=0)
        scores = [[] for _ in range(group)]

        def pick(ref, start, e):
            return jnp.concatenate([ref[picks[start + e]], ref[picks[start + e + 1]]], axis=0)

        def put(r, e, s):
            for d in range(2):
                block = s[:, d * BLK : (d + 1) * BLK]
                if e + d == 0:
                    block = jnp.where(triangle, block, masked_score)
                else:
                    block = block + biases[base[r] + e + d]
                scores[r].append(block)

        for e in range(0, 4, 2):
            for r in range(group):
                s = lax.dot_general(q[r], pick(keys, base[r], e), dims, preferred_element_type=jnp.float32)
                put(r, e, s)
        for e in range(4, NLIST, 2):
            s = lax.dot_general(q_all, pick(keys, base[0], e), dims, preferred_element_type=jnp.float32)
            for r in range(group):
                put(r, e, s[r * HALF : (r + 1) * HALF])
        weights = []
        inverse = []
        for r in range(group):
            top = functools.reduce(jnp.maximum, scores[r] if exact else scores[r][:4])
            top = jnp.max(top, axis=1, keepdims=True) * SCALE
            w = [jnp.exp2(s * SCALE - top) for s in scores[r]]
            total = functools.reduce(jnp.add, w)
            largest = jnp.maximum(largest, total)
            inverse.append(1.0 / jnp.sum(total, axis=1, keepdims=True))
            weights.append([a.astype(jnp.bfloat16) for a in w])
        summed = []
        for r in range(group):
            acc = jnp.zeros((HALF, DH), jnp.float32)
            for e in range(0, 4, 2):
                pair = jnp.concatenate(weights[r][e : e + 2], axis=1)
                acc = acc + jnp.dot(pair, pick(values, base[r], e), preferred_element_type=jnp.float32)
            summed.append(acc)
        acc = jnp.concatenate(summed, axis=0)
        for e in range(4, NLIST, 2):
            pair = jnp.concatenate(
                [jnp.concatenate(weights[r][e : e + 2], axis=1) for r in range(group)], axis=0
            )
            acc = acc + jnp.dot(pair, pick(values, base[0], e), preferred_element_type=jnp.float32)
        for r in range(group):
            result = acc[r * HALF : (r + 1) * HALF] * inverse[r]
            out_ref[part * group + r, :, lane] = result.astype(jnp.bfloat16)
        return largest

    return lax.fori_loop(0, GROUP * 8 // group, step, jnp.zeros((HALF, BLK), jnp.float32))


def attention_kernel(place, picks, biases, q_ref, cached, span, out_ref, kbuf, vbuf, sems):
    zl = place[5]
    copies = []

    def copy(source, target):
        copies.append(pltpu.make_async_copy(source, target, sems.at[len(copies)]))

    for i, buffer in enumerate((kbuf, vbuf)):
        for slot in range(32):
            x, k, y = slot // 8, slot // 4 % 2, slot % 4
            copy(cached.at[slot, 0, i], buffer.at[0, x, zl, k, y])
            copy(cached.at[slot, 1, i], buffer.at[0, x, 1 - zl, k, y])
            rows = pl.ds(y % 2 * HALF, HALF)
            copy(span.at[slot, 2:, i], buffer.at[1, x, :, k, :, y // 2, rows, :])
    for entry in copies:
        entry.start()
    for entry in copies:
        entry.wait()

    keys = kbuf.reshape(256, BLK, DH)
    values = vbuf.reshape(256, BLK, DH)
    largest = attend(False, place, picks, biases, q_ref, keys, values, out_ref)

    @pl.when(jnp.logical_not(jnp.max(largest) < LARGEST))
    def _():
        attend(True, place, picks, biases, q_ref, keys, values, out_ref)


def attention(place, picks, biases, queries, gathered):
    return pl.pallas_call(
        attention_kernel,
        out_shape=shaped((8, HALF, GROUP * DH)),
        in_specs=[SMEM, SMEM, SMEM, VMEM, HBM, HBM],
        out_specs=VMEM,
        scratch_shapes=[
            pltpu.VMEM(BUFFER, jnp.bfloat16),
            pltpu.VMEM(BUFFER, jnp.bfloat16),
            pltpu.SemaphoreType.DMA((192,)),
        ],
        compiler_params=pltpu.CompilerParams(vmem_limit_bytes=56 * 1024 * 1024),
        cost_estimate=pl.CostEstimate(
            flops=2 * 2 * GROUP * 512 * 2560 * 128,
            bytes_accessed=18 << 20,
            transcendentals=GROUP * 512 * 2560,
        ),
        name="attention",
    )(
        place,
        picks,
        biases,
        queries,
        gathered.reshape(32, 4, 2, 2, BLK, DH),
        gathered.reshape(32, 4, 2, 4, HALF, DH),
    )


def head_table(around, my_y, zl):
    origins = (my_y + jnp.array([0, 3, 1, 2], jnp.int32)) % 4

    def of(wanted):
        return jnp.sum(jnp.where((origins == wanted)[:, None, None], around, 0), axis=0)

    return jnp.concatenate([of(2 * zl), of(2 * zl + 1)], axis=0)


def listed_blocks(table, my_x, my_y, my_k):
    verticals, slashes = table[:, :16], table[:, 16:]
    shard = jnp.arange(16, dtype=jnp.int32)
    vertical = shard * 8 + verticals + jnp.where(verticals >= 8, 120, 0)
    zl = jnp.arange(8, dtype=jnp.int32) // 4
    zh = jnp.arange(8, dtype=jnp.int32) % 4
    own = 128 + (my_x * 4 + zl * 2 + my_k) * 8 + zh * 2 + my_y // 2
    target = own[None, :, None] - slashes[:, None, :]
    before = jnp.arange(3)[None, :] < jnp.arange(3)[:, None]
    repeated = jnp.any((slashes[:, :, None] == slashes[:, None, :]) & before, axis=-1)
    listed = jnp.any(target[..., None] == vertical[:, None, None, :], axis=-1)
    slash_ok = (target >= 0) & jnp.logical_not(repeated[:, None, :]) & jnp.logical_not(listed)
    vertical_ok = vertical[:, None, :] < own[None, :, None]
    shape = (GROUP, 8, 1)
    picks = jnp.concatenate(
        [
            jnp.broadcast_to(own[None, :, None], shape),
            jnp.maximum(target, 0),
            jnp.broadcast_to(vertical[:, None, :], (GROUP, 8, 16)),
        ],
        axis=2,
    )
    usable = jnp.concatenate([jnp.ones(shape, bool), slash_ok, vertical_ok], axis=2)
    biases = jnp.where(usable, 0.0, masked_score).astype(jnp.float32)
    return picks.reshape(-1), biases.reshape(-1)


def per_device(queries, span_keys, span_values, cache_keys, cache_values, verticals, slashes):
    my_x, my_y, my_k = lax.axis_index("x"), lax.axis_index("y"), lax.axis_index("k")
    zh, zl = lax.axis_index("zh"), lax.axis_index("zl")
    plane = zh * 2 + zl
    zaxes = ("zl", "zh")

    table = jnp.concatenate([verticals[:, :, 0], slashes], axis=1)
    table = head_table(jnp.stack(ring_direct(table, "y")), my_y, zl)
    place = jnp.stack([my_x, my_y, my_k, plane, plane + 1 - 2 * zl, zl]).astype(jnp.int32)

    own, other, span = payload(place, cache_keys, cache_values, span_keys, span_values)
    swapped = shift(other, "zl", 2, 1)
    span = lax.all_to_all(span, zaxes, split_axis=0, concat_axis=0, tiled=True)
    packed = pack(own, swapped, span)
    gathered = lax.all_gather(packed, ("x", "k", "y"), axis=0, tiled=False)
    slab_queries = lax.all_to_all(
        by_plane(queries, (packed,)), zaxes, split_axis=0, concat_axis=0, tiled=True
    )
    picks, biases = listed_blocks(table, my_x, my_y, my_k)

    attended = attention(place, picks, biases, slab_queries, gathered)
    result = lax.all_to_all(attended, zaxes, split_axis=0, concat_axis=0, tiled=True)
    return jnp.concatenate([result[PLANES.index(p)] for p in range(8)], axis=1)


def solution(mesh):
    axes = ("x", "zl", "k", "zh", "y")
    fine = Mesh(np.asarray(mesh.devices).reshape(4, 2, 2, 4, 4), axes)
    rows = P(axes, None)
    return jax.shard_map(
        per_device,
        mesh=fine,
        in_specs=(
            rows,
            rows,
            rows,
            P(("x", "zl", "k"), None),
            P(("x", "zl", "k"), None),
            P(("zh", "y"), None, None),
            P(("zh", "y"), None),
        ),
        out_specs=rows,
        check_vma=False,
    )
```

```python
import functools

import jax
import jax.numpy as jnp
import numpy as np
from jax import lax
from jax.experimental import pallas as pl
from jax.experimental.pallas import tpu as pltpu
from jax.sharding import Mesh
from jax.sharding import PartitionSpec as P

H = 64
KVH = 8
DH = 128
BLK = 128
GROUP = H // KVH
HALF = 64
NLIST = 20
masked_score = -1e30
SCALE = DH ** (-0.5) * 1.4426950408889634


def shift(value, axis, size, step):
    return lax.ppermute(value, axis, [(i, (i + step) % size) for i in range(size)])


def ring_direct(value, axis):
    return [value, shift(value, axis, 4, 1), shift(value, axis, 4, -1), shift(value, axis, 4, 2)]


ORIGINS = (0, -1, 1, 2)
PLANES = (0, 2, 4, 6, 1, 3, 5, 7)


HBM = pl.BlockSpec(memory_space=pltpu.HBM)
SMEM = pl.BlockSpec(memory_space=pltpu.SMEM)
VMEM = pl.BlockSpec(memory_space=pltpu.VMEM)


def shaped(shape, dtype=jnp.bfloat16):
    return jax.ShapeDtypeStruct(shape, dtype)


def slab_copies(cache_keys, cache_values, plane, target, sems):
    lanes = pl.ds(pl.multiple_of(plane * DH, DH), DH)
    return [
        pltpu.make_async_copy(cache.at[:, lanes], target.at[i], sems.at[i])
        for i, cache in enumerate((cache_keys, cache_values))
    ]


def payload_kernel(place, cache_keys, cache_values, span_keys, span_values, own, span, sems):
    copies = slab_copies(cache_keys, cache_values, place[3], own, sems)
    for copy in copies:
        copy.start()
    for i, source in enumerate((span_keys, span_values)):
        for slot, p in enumerate(PLANES):
            span[slot, i] = source[:, p * DH : (p + 1) * DH]
    for copy in copies:
        copy.wait()


def payload(place, cache_keys, cache_values, span_keys, span_values):
    return pl.pallas_call(
        payload_kernel,
        out_shape=[shaped((2, cache_keys.shape[0], DH)), shaped((8, 2, HALF, DH))],
        in_specs=[SMEM, HBM, HBM, VMEM, VMEM],
        out_specs=[VMEM, VMEM],
        scratch_shapes=[pltpu.SemaphoreType.DMA((2,))],
        compiler_params=pltpu.CompilerParams(vmem_limit_bytes=56 * 1024 * 1024),
        name="payload",
    )(place, cache_keys, cache_values, span_keys, span_values)


def neighbour_kernel(place, cache_keys, cache_values, after, other, sems):
    copies = slab_copies(cache_keys, cache_values, place[4], other, sems)
    for copy in copies:
        copy.start()
    for copy in copies:
        copy.wait()


def neighbour(place, cache_keys, cache_values, after):
    return pl.pallas_call(
        neighbour_kernel,
        out_shape=shaped((2, cache_keys.shape[0], DH)),
        in_specs=[SMEM, HBM, HBM, HBM],
        out_specs=VMEM,
        scratch_shapes=[pltpu.SemaphoreType.DMA((2,))],
        compiler_params=pltpu.CompilerParams(vmem_limit_bytes=56 * 1024 * 1024),
        name="neighbour",
    )(place, cache_keys, cache_values, after)


def split_kernel(span, table, keys, values):
    for slot in range(8):
        keys[slot * HALF : (slot + 1) * HALF] = span[slot, 0]
        values[slot * HALF : (slot + 1) * HALF] = span[slot, 1]
    values[8 * HALF :] = table[...]


def split(span, table):
    return pl.pallas_call(
        split_kernel,
        out_shape=[shaped((8 * HALF, DH)), shaped((8 * HALF + 16, DH))],
        in_specs=[VMEM, VMEM],
        out_specs=[VMEM, VMEM],
        name="split",
    )(span, table)


def stack_kernel(*refs):
    keys, values, tables = refs[8:]
    for slot in range(4):
        keys[slot] = refs[slot][...]
        values[slot] = refs[4 + slot][: 8 * HALF]
        tables[slot] = refs[4 + slot][8 * HALF :]


def stack(keys, values):
    return pl.pallas_call(
        stack_kernel,
        out_shape=[shaped((4, 8 * HALF, DH))] * 2 + [shaped((4, 16, DH))],
        in_specs=[VMEM] * 8,
        out_specs=[VMEM] * 3,
        name="stack",
    )(*keys, *values)


def plane_kernel(extra, source, *refs):
    target = refs[extra]
    width = GROUP * DH
    for slot, plane in enumerate(PLANES):
        target[slot] = source[:, plane * width : (plane + 1) * width]


def by_plane(queries, after=()):
    return pl.pallas_call(
        functools.partial(plane_kernel, len(after)),
        out_shape=shaped((8, HALF, GROUP * DH)),
        in_specs=[VMEM] + [HBM] * len(after),
        out_specs=VMEM,
        name="by_plane",
    )(queries, *after)


def second_stage(plan, arrays, slots, is_value):
    x_first = not is_value
    axis = "y" if x_first else "x"
    left, right = shift(slots, axis, 4, 1), shift(slots, axis, 4, -1)
    pieces = [slots, left, right, shift(left, axis, 4, 1)]
    for array, origin in zip(pieces, ORIGINS):
        for other in range(2):
            plan.append((is_value, x_first, origin, other))
            arrays.append((shift(array, "k", 2, 1) if other else array).reshape(4, 2, 4, HALF, DH))


BUFFER = (2, 4, 2, 2, 4, 2, BLK, DH)


LARGEST = 2.0**90


def attend(exact, place, picks, biases, q_ref, keys, values, out_ref):
    group = 4 if exact else 8
    half = lax.rem(place[1], 2) * HALF
    rows = lax.broadcasted_iota(jnp.int32, (HALF, BLK), 0) + half
    cols = lax.broadcasted_iota(jnp.int32, (HALF, BLK), 1)
    triangle = cols <= rows
    dims = (((1,), (1,)), ((), ()))

    def step(item, largest):
        head = lax.div(item, 8 // group)
        part = lax.rem(item, 8 // group)
        lane = pl.ds(pl.multiple_of(head * DH, DH), DH)
        base = [(head * 8 + part * group + r) * NLIST for r in range(group)]
        q = [q_ref[part * group + r, :, lane] for r in range(group)]
        q_all = jnp.concatenate(q, axis=0)
        scores = [[] for _ in range(group)]

        def pick(ref, start, e):
            return jnp.concatenate([ref[picks[start + e]], ref[picks[start + e + 1]]], axis=0)

        def put(r, e, s):
            for d in range(2):
                block = s[:, d * BLK : (d + 1) * BLK]
                if e + d == 0:
                    block = jnp.where(triangle, block, masked_score)
                else:
                    block = block + biases[base[r] + e + d]
                scores[r].append(block)

        for e in range(0, 4, 2):
            for r in range(group):
                s = lax.dot_general(q[r], pick(keys, base[r], e), dims, preferred_element_type=jnp.float32)
                put(r, e, s)
        for e in range(4, NLIST, 2):
            s = lax.dot_general(q_all, pick(keys, base[0], e), dims, preferred_element_type=jnp.float32)
            for r in range(group):
                put(r, e, s[r * HALF : (r + 1) * HALF])
        weights = []
        inverse = []
        for r in range(group):
            top = functools.reduce(jnp.maximum, scores[r] if exact else scores[r][:4])
            top = jnp.max(top, axis=1, keepdims=True) * SCALE
            w = [jnp.exp2(s * SCALE - top) for s in scores[r]]
            total = functools.reduce(jnp.add, w)
            largest = jnp.maximum(largest, total)
            inverse.append(1.0 / jnp.sum(total, axis=1, keepdims=True))
            weights.append([a.astype(jnp.bfloat16) for a in w])
        summed = []
        for r in range(group):
            acc = jnp.zeros((HALF, DH), jnp.float32)
            for e in range(0, 4, 2):
                pair = jnp.concatenate(weights[r][e : e + 2], axis=1)
                acc = acc + jnp.dot(pair, pick(values, base[r], e), preferred_element_type=jnp.float32)
            summed.append(acc)
        acc = jnp.concatenate(summed, axis=0)
        for e in range(4, NLIST, 2):
            pair = jnp.concatenate(
                [jnp.concatenate(weights[r][e : e + 2], axis=1) for r in range(group)], axis=0
            )
            acc = acc + jnp.dot(pair, pick(values, base[0], e), preferred_element_type=jnp.float32)
        for r in range(group):
            result = acc[r * HALF : (r + 1) * HALF] * inverse[r]
            out_ref[part * group + r, :, lane] = result.astype(jnp.bfloat16)
        return largest

    return lax.fori_loop(0, GROUP * 8 // group, step, jnp.zeros((HALF, BLK), jnp.float32))


def attention_kernel(plan, place, picks, biases, q_ref, own, other, *refs):
    pieces = refs[: len(plan)]
    out_ref, kbuf, vbuf, sems = refs[len(plan) :]
    my_x, my_y, my_k, zl = place[0], place[1], place[2], place[5]
    copies = []

    def copy(source, target):
        copies.append(pltpu.make_async_copy(source, target, sems.at[len(copies)]))

    for slot in range(8):
        for i, buffer in enumerate((kbuf, vbuf)):
            copy(own.at[slot, i], buffer.at[0, slot // 2, zl, slot % 2])
            copy(other.at[slot, i], buffer.at[0, slot // 2, 1 - zl, slot % 2])
    for piece, (is_value, x_first, origin, other_k) in zip(pieces, plan):
        buffer = vbuf if is_value else kbuf
        for slot, near in enumerate(ORIGINS):
            dx, dy = (near, origin) if x_first else (origin, near)
            from_x = lax.rem(my_x + (dx + 4), 4)
            from_y = lax.rem(my_y + (dy + 4), 4)
            from_k = 1 - my_k if other_k else my_k
            rows = pl.ds(pl.multiple_of(lax.rem(from_y, 2) * HALF, HALF), HALF)
            copy(piece.at[slot], buffer.at[1, from_x, :, from_k, :, lax.div(from_y, 2), rows, :])
    for entry in copies:
        entry.start()
    for entry in copies:
        entry.wait()

    keys = kbuf.reshape(256, BLK, DH)
    values = vbuf.reshape(256, BLK, DH)
    largest = attend(False, place, picks, biases, q_ref, keys, values, out_ref)

    @pl.when(jnp.logical_not(jnp.max(largest) < LARGEST))
    def _():
        attend(True, place, picks, biases, q_ref, keys, values, out_ref)


def attention(plan, place, picks, biases, queries, own, other, pieces):
    return pl.pallas_call(
        functools.partial(attention_kernel, tuple(plan)),
        out_shape=shaped((8, HALF, GROUP * DH)),
        in_specs=[SMEM, SMEM, SMEM, VMEM] + [HBM] * (2 + len(pieces)),
        out_specs=VMEM,
        scratch_shapes=[
            pltpu.VMEM(BUFFER, jnp.bfloat16),
            pltpu.VMEM(BUFFER, jnp.bfloat16),
            pltpu.SemaphoreType.DMA((32 + 4 * len(pieces),)),
        ],
        compiler_params=pltpu.CompilerParams(vmem_limit_bytes=56 * 1024 * 1024),
        cost_estimate=pl.CostEstimate(
            flops=2 * 2 * GROUP * 512 * 2560 * 128,
            bytes_accessed=18 << 20,
            transcendentals=GROUP * 512 * 2560,
        ),
        name="attention",
    )(place, picks, biases, queries, own, other, *pieces)


def head_table(around, my_y, zl):
    origins = (my_y + jnp.array([0, 3, 1, 2], jnp.int32)) % 4

    def of(wanted):
        return jnp.sum(jnp.where((origins == wanted)[:, None, None], around, 0), axis=0)

    return jnp.concatenate([of(2 * zl), of(2 * zl + 1)], axis=0)


def listed_blocks(table, my_x, my_y, my_k):
    verticals, slashes = table[:, :16], table[:, 16:]
    shard = jnp.arange(16, dtype=jnp.int32)
    vertical = shard * 8 + verticals + jnp.where(verticals >= 8, 120, 0)
    zl = jnp.arange(8, dtype=jnp.int32) // 4
    zh = jnp.arange(8, dtype=jnp.int32) % 4
    own = 128 + (my_x * 4 + zl * 2 + my_k) * 8 + zh * 2 + my_y // 2
    target = own[None, :, None] - slashes[:, None, :]
    before = jnp.arange(3)[None, :] < jnp.arange(3)[:, None]
    repeated = jnp.any((slashes[:, :, None] == slashes[:, None, :]) & before, axis=-1)
    listed = jnp.any(target[..., None] == vertical[:, None, None, :], axis=-1)
    slash_ok = (target >= 0) & jnp.logical_not(repeated[:, None, :]) & jnp.logical_not(listed)
    vertical_ok = vertical[:, None, :] < own[None, :, None]
    shape = (GROUP, 8, 1)
    picks = jnp.concatenate(
        [
            jnp.broadcast_to(own[None, :, None], shape),
            jnp.maximum(target, 0),
            jnp.broadcast_to(vertical[:, None, :], (GROUP, 8, 16)),
        ],
        axis=2,
    )
    usable = jnp.concatenate([jnp.ones(shape, bool), slash_ok, vertical_ok], axis=2)
    biases = jnp.where(usable, 0.0, masked_score).astype(jnp.float32)
    return picks.reshape(-1), biases.reshape(-1)


def per_device(queries, span_keys, span_values, cache_keys, cache_values, verticals, slashes):
    my_x, my_y, my_k = lax.axis_index("x"), lax.axis_index("y"), lax.axis_index("k")
    zh, zl = lax.axis_index("zh"), lax.axis_index("zl")
    plane = zh * 2 + zl
    zaxes = ("zl", "zh")

    table = jnp.concatenate([verticals[:, :, 0], slashes], axis=1).astype(jnp.bfloat16)
    table = jnp.pad(table, ((0, 12), (0, DH - 19)))
    place = jnp.stack([my_x, my_y, my_k, plane, plane + 1 - 2 * zl, zl]).astype(jnp.int32)

    own, span = payload(place, cache_keys, cache_values, span_keys, span_values)
    span = lax.all_to_all(span, zaxes, split_axis=0, concat_axis=0, tiled=True)

    def slabs(slab):
        held = lax.all_gather(slab, ("x", "k"), axis=0, tiled=False)
        return held.reshape(8, 2, 4, 2, BLK, DH)

    span_k, span_v = split(span, table)
    span_k, span_v = ring_direct(span_k, "x"), ring_direct(span_v, "y")
    swapped = shift(neighbour(place, cache_keys, cache_values, span_k[1]), "zl", 2, 1)
    own, swapped = slabs(own), slabs(swapped)
    slab_queries = lax.all_to_all(
        by_plane(queries, (span_k[1],)), zaxes, split_axis=0, concat_axis=0, tiled=True
    )
    span_k, span_v, tables = stack(span_k, span_v)
    table = head_table(tables[:, :4, :19].astype(jnp.int32), my_y, zl)
    plan = []
    pieces = []
    second_stage(plan, pieces, span_k, False)
    second_stage(plan, pieces, span_v, True)
    picks, biases = listed_blocks(table, my_x, my_y, my_k)
    attended = attention(plan, place, picks, biases, slab_queries, own, swapped, pieces)
    result = lax.all_to_all(attended, zaxes, split_axis=0, concat_axis=0, tiled=True)
    return jnp.concatenate([result[PLANES.index(p)] for p in range(8)], axis=1)


def solution(mesh):
    axes = ("x", "zl", "k", "zh", "y")
    fine = Mesh(np.asarray(mesh.devices).reshape(4, 2, 2, 4, 4), axes)
    rows = P(axes, None)
    return jax.shard_map(
        per_device,
        mesh=fine,
        in_specs=(
            rows,
            rows,
            rows,
            P(("x", "zl", "k"), None),
            P(("x", "zl", "k"), None),
            P(("zh", "y"), None, None),
            P(("zh", "y"), None),
        ),
        out_specs=rows,
        check_vma=False,
    )
```

```python
import functools

import jax
import jax.numpy as jnp
import numpy as np
from jax import lax
from jax.experimental import pallas as pl
from jax.experimental.pallas import tpu as pltpu
from jax.sharding import Mesh
from jax.sharding import PartitionSpec as P

H = 64
KVH = 8
DH = 128
BLK = 128
GROUP = H // KVH
HALF = 64
NLIST = 20
LARGEST = 2.0**90
masked_score = -1e30
SCALE = DH ** (-0.5) * 1.4426950408889634


def shift(value, axis, size, step):
    return lax.ppermute(value, axis, [(i, (i + step) % size) for i in range(size)])


def ring_direct(value, axis):
    return [value, shift(value, axis, 4, 1), shift(value, axis, 4, -1), shift(value, axis, 4, 2)]


ORIGINS = (0, -1, 1, 2)
PLANES = (0, 2, 4, 6, 1, 3, 5, 7)


HBM = pl.BlockSpec(memory_space=pltpu.HBM)
SMEM = pl.BlockSpec(memory_space=pltpu.SMEM)
VMEM = pl.BlockSpec(memory_space=pltpu.VMEM)


def shaped(shape, dtype=jnp.bfloat16):
    return jax.ShapeDtypeStruct(shape, dtype)


def payload_kernel(place, cache_keys, cache_values, span_keys, span_values, own, other, span, sems):
    start = pl.multiple_of(place[1] * 256, 256)
    copies = []
    for i, cache in enumerate((cache_keys, cache_values)):
        for j, (target, column) in enumerate(((own, place[3]), (other, place[4]))):
            lanes = pl.ds(pl.multiple_of(column * DH, DH), DH)
            copies.append(
                pltpu.make_async_copy(cache.at[pl.ds(start, 256), lanes], target.at[i], sems.at[2 * i + j])
            )
    for copy in copies:
        copy.start()
    for i, source in enumerate((span_keys, span_values)):
        for slot, p in enumerate(PLANES):
            span[slot, i] = source[:, p * DH : (p + 1) * DH]
    for copy in copies:
        copy.wait()


def payload(place, cache_keys, cache_values, span_keys, span_values):
    return pl.pallas_call(
        payload_kernel,
        out_shape=[shaped((2, 256, DH)), shaped((2, 256, DH)), shaped((8, 2, HALF, DH))],
        in_specs=[SMEM, HBM, HBM, VMEM, VMEM],
        out_specs=[VMEM, VMEM, VMEM],
        scratch_shapes=[pltpu.SemaphoreType.DMA((4,))],
        compiler_params=pltpu.CompilerParams(vmem_limit_bytes=56 * 1024 * 1024),
        name="payload",
    )(place, cache_keys, cache_values, span_keys, span_values)


def pack_kernel(own, swapped, span, out, low, high):
    for i in range(2):
        out[i] = own[i]
        out[2 + i] = swapped[i]
        for zh in range(4):
            rows = slice(zh * HALF, (zh + 1) * HALF)
            out[4 + i, rows] = span[i * 4 + zh, 1]
            (low, high)[i][rows] = span[i * 4 + zh, 0]


def pack(own, swapped, span):
    return pl.pallas_call(
        pack_kernel,
        out_shape=[shaped((6, 256, DH)), shaped((256, DH)), shaped((256, DH))],
        in_specs=[VMEM] * 3,
        out_specs=[VMEM] * 3,
        name="pack",
    )(own, swapped, span)


def stack_kernel(*refs):
    for i, source in enumerate(refs[:8]):
        refs[8 + i // 4][i % 4] = source[...]


def stack(low, high):
    return pl.pallas_call(
        stack_kernel,
        out_shape=[shaped((4, 256, DH))] * 2,
        in_specs=[VMEM] * 8,
        out_specs=[VMEM] * 2,
        name="stack",
    )(*low, *high)


def second_stage(plan, arrays, slots, from_zl):
    axis = "x" if from_zl else "y"
    left, right = shift(slots, axis, 4, 1), shift(slots, axis, 4, -1)
    pieces = [slots, left, right, shift(left, axis, 4, 1)]
    for array, origin in zip(pieces, ORIGINS):
        for other in range(2):
            plan.append((from_zl, origin, other))
            arrays.append((shift(array, "k", 2, 1) if other else array).reshape(4, 4, HALF, DH))


def plane_kernel(extra, source, *refs):
    target = refs[extra]
    width = GROUP * DH
    for slot, plane in enumerate(PLANES):
        target[slot] = source[:, plane * width : (plane + 1) * width]


def by_plane(queries, after=()):
    return pl.pallas_call(
        functools.partial(plane_kernel, len(after)),
        out_shape=shaped((8, HALF, GROUP * DH)),
        in_specs=[VMEM] + [HBM] * len(after),
        out_specs=VMEM,
        name="by_plane",
    )(queries, *after)


BUFFER = (2, 4, 2, 2, 4, 2, BLK, DH)


def attend(exact, place, picks, biases, q_ref, keys, values, out_ref):
    group = 4 if exact else 8
    half = lax.rem(place[1], 2) * HALF
    rows = lax.broadcasted_iota(jnp.int32, (HALF, BLK), 0) + half
    cols = lax.broadcasted_iota(jnp.int32, (HALF, BLK), 1)
    triangle = cols <= rows
    dims = (((1,), (1,)), ((), ()))

    def step(item, largest):
        head = lax.div(item, 8 // group)
        part = lax.rem(item, 8 // group)
        lane = pl.ds(pl.multiple_of(head * DH, DH), DH)
        base = [(head * 8 + part * group + r) * NLIST for r in range(group)]
        q = [q_ref[part * group + r, :, lane] for r in range(group)]
        q_all = jnp.concatenate(q, axis=0)
        scores = [[] for _ in range(group)]

        def pick(ref, start, e):
            return jnp.concatenate([ref[picks[start + e]], ref[picks[start + e + 1]]], axis=0)

        def put(r, e, s):
            for d in range(2):
                block = s[:, d * BLK : (d + 1) * BLK]
                if e + d == 0:
                    block = jnp.where(triangle, block, masked_score)
                else:
                    block = block + biases[base[r] + e + d]
                scores[r].append(block)

        for e in range(0, 4, 2):
            for r in range(group):
                s = lax.dot_general(q[r], pick(keys, base[r], e), dims, preferred_element_type=jnp.float32)
                put(r, e, s)
        for e in range(4, NLIST, 2):
            s = lax.dot_general(q_all, pick(keys, base[0], e), dims, preferred_element_type=jnp.float32)
            for r in range(group):
                put(r, e, s[r * HALF : (r + 1) * HALF])
        weights = []
        inverse = []
        for r in range(group):
            top = functools.reduce(jnp.maximum, scores[r] if exact else scores[r][:4])
            top = jnp.max(top, axis=1, keepdims=True) * SCALE
            w = [jnp.exp2(s * SCALE - top) for s in scores[r]]
            total = functools.reduce(jnp.add, w)
            largest = jnp.maximum(largest, total)
            inverse.append(1.0 / jnp.sum(total, axis=1, keepdims=True))
            weights.append([a.astype(jnp.bfloat16) for a in w])
        summed = []
        for r in range(group):
            acc = jnp.zeros((HALF, DH), jnp.float32)
            for e in range(0, 4, 2):
                pair = jnp.concatenate(weights[r][e : e + 2], axis=1)
                acc = acc + jnp.dot(pair, pick(values, base[r], e), preferred_element_type=jnp.float32)
            summed.append(acc)
        acc = jnp.concatenate(summed, axis=0)
        for e in range(4, NLIST, 2):
            pair = jnp.concatenate(
                [jnp.concatenate(weights[r][e : e + 2], axis=1) for r in range(group)], axis=0
            )
            acc = acc + jnp.dot(pair, pick(values, base[0], e), preferred_element_type=jnp.float32)
        for r in range(group):
            result = acc[r * HALF : (r + 1) * HALF] * inverse[r]
            out_ref[part * group + r, :, lane] = result.astype(jnp.bfloat16)
        return largest

    return lax.fori_loop(0, GROUP * 8 // group, step, jnp.zeros((HALF, BLK), jnp.float32))


def attention_kernel(plan, place, picks, biases, q_ref, cached, span, *refs):
    pieces = refs[: len(plan)]
    out_ref, kbuf, vbuf, sems = refs[len(plan) :]
    my_x, my_y, my_k, zl = place[0], place[1], place[2], place[5]
    copies = []

    def copy(source, target):
        copies.append(pltpu.make_async_copy(source, target, sems.at[len(copies)]))

    for piece, (from_zl, origin, other) in zip(pieces, plan):
        for slot, near in enumerate(ORIGINS):
            dx, dy = (origin, near) if from_zl else (near, origin)
            from_x = lax.rem(my_x + (dx + 4), 4)
            from_y = lax.rem(my_y + (dy + 4), 4)
            from_k = 1 - my_k if other else my_k
            rows = pl.ds(pl.multiple_of(lax.rem(from_y, 2) * HALF, HALF), HALF)
            copy(piece.at[slot], kbuf.at[1, from_x, from_zl, from_k, :, lax.div(from_y, 2), rows, :])
    for slot in range(32):
        x, k, y = slot // 8, slot // 4 % 2, slot % 4
        for i, buffer in enumerate((kbuf, vbuf)):
            copy(cached.at[slot, i], buffer.at[0, x, zl, k, y])
            copy(cached.at[slot, 2 + i], buffer.at[0, x, 1 - zl, k, y])
        copy(span.at[slot, 4:], vbuf.at[1, x, :, k, :, y // 2, pl.ds(y % 2 * HALF, HALF), :])
    for entry in copies:
        entry.start()
    for entry in copies:
        entry.wait()

    keys = kbuf.reshape(256, BLK, DH)
    values = vbuf.reshape(256, BLK, DH)
    largest = attend(False, place, picks, biases, q_ref, keys, values, out_ref)

    @pl.when(jnp.logical_not(jnp.max(largest) < LARGEST))
    def _():
        attend(True, place, picks, biases, q_ref, keys, values, out_ref)


def attention(plan, place, picks, biases, queries, gathered, pieces):
    return pl.pallas_call(
        functools.partial(attention_kernel, tuple(plan)),
        out_shape=shaped((8, HALF, GROUP * DH)),
        in_specs=[SMEM, SMEM, SMEM, VMEM, HBM, HBM] + [HBM] * len(pieces),
        out_specs=VMEM,
        scratch_shapes=[
            pltpu.VMEM(BUFFER, jnp.bfloat16),
            pltpu.VMEM(BUFFER, jnp.bfloat16),
            pltpu.SemaphoreType.DMA((160 + 4 * len(pieces),)),
        ],
        compiler_params=pltpu.CompilerParams(vmem_limit_bytes=56 * 1024 * 1024),
        cost_estimate=pl.CostEstimate(
            flops=2 * 2 * GROUP * 512 * 2560 * 128,
            bytes_accessed=18 << 20,
            transcendentals=GROUP * 512 * 2560,
        ),
        name="attention",
    )(
        place,
        picks,
        biases,
        queries,
        gathered.reshape(32, 6, 2, BLK, DH),
        gathered.reshape(32, 6, 4, HALF, DH),
        *pieces,
    )


def head_table(around, my_y, zl):
    origins = (my_y + jnp.array([0, 3, 1, 2], jnp.int32)) % 4

    def of(wanted):
        return jnp.sum(jnp.where((origins == wanted)[:, None, None], around, 0), axis=0)

    return jnp.concatenate([of(2 * zl), of(2 * zl + 1)], axis=0)


def listed_blocks(table, my_x, my_y, my_k):
    verticals, slashes = table[:, :16], table[:, 16:]
    shard = jnp.arange(16, dtype=jnp.int32)
    vertical = shard * 8 + verticals + jnp.where(verticals >= 8, 120, 0)
    zl = jnp.arange(8, dtype=jnp.int32) // 4
    zh = jnp.arange(8, dtype=jnp.int32) % 4
    own = 128 + (my_x * 4 + zl * 2 + my_k) * 8 + zh * 2 + my_y // 2
    target = own[None, :, None] - slashes[:, None, :]
    before = jnp.arange(3)[None, :] < jnp.arange(3)[:, None]
    repeated = jnp.any((slashes[:, :, None] == slashes[:, None, :]) & before, axis=-1)
    listed = jnp.any(target[..., None] == vertical[:, None, None, :], axis=-1)
    slash_ok = (target >= 0) & jnp.logical_not(repeated[:, None, :]) & jnp.logical_not(listed)
    vertical_ok = vertical[:, None, :] < own[None, :, None]
    shape = (GROUP, 8, 1)
    picks = jnp.concatenate(
        [
            jnp.broadcast_to(own[None, :, None], shape),
            jnp.maximum(target, 0),
            jnp.broadcast_to(vertical[:, None, :], (GROUP, 8, 16)),
        ],
        axis=2,
    )
    usable = jnp.concatenate([jnp.ones(shape, bool), slash_ok, vertical_ok], axis=2)
    biases = jnp.where(usable, 0.0, masked_score).astype(jnp.float32)
    return picks.reshape(-1), biases.reshape(-1)


def per_device(queries, span_keys, span_values, cache_keys, cache_values, verticals, slashes):
    my_x, my_y, my_k = lax.axis_index("x"), lax.axis_index("y"), lax.axis_index("k")
    zh, zl = lax.axis_index("zh"), lax.axis_index("zl")
    plane = zh * 2 + zl
    zaxes = ("zl", "zh")

    table = jnp.concatenate([verticals[:, :, 0], slashes], axis=1)
    table = head_table(jnp.stack(ring_direct(table, "y")), my_y, zl)
    place = jnp.stack([my_x, my_y, my_k, plane, plane + 1 - 2 * zl, zl]).astype(jnp.int32)

    own, other, span = payload(place, cache_keys, cache_values, span_keys, span_values)
    swapped = shift(other, "zl", 2, 1)
    span = lax.all_to_all(span, zaxes, split_axis=0, concat_axis=0, tiled=True)
    packed, low, high = pack(own, swapped, span)
    gathered = lax.all_gather(packed, ("x", "k", "y"), axis=0, tiled=False)
    slab_queries = lax.all_to_all(
        by_plane(queries, (low,)), zaxes, split_axis=0, concat_axis=0, tiled=True
    )
    picks, biases = listed_blocks(table, my_x, my_y, my_k)

    low, high = stack(ring_direct(low, "x"), ring_direct(high, "y"))
    plan = []
    pieces = []
    second_stage(plan, pieces, low, 0)
    second_stage(plan, pieces, high, 1)
    attended = attention(plan, place, picks, biases, slab_queries, gathered, pieces)
    result = lax.all_to_all(attended, zaxes, split_axis=0, concat_axis=0, tiled=True)
    return jnp.concatenate([result[PLANES.index(p)] for p in range(8)], axis=1)


def solution(mesh):
    axes = ("x", "zl", "k", "zh", "y")
    fine = Mesh(np.asarray(mesh.devices).reshape(4, 2, 2, 4, 4), axes)
    rows = P(axes, None)
    return jax.shard_map(
        per_device,
        mesh=fine,
        in_specs=(
            rows,
            rows,
            rows,
            P(("x", "zl", "k"), None),
            P(("x", "zl", "k"), None),
            P(("zh", "y"), None, None),
            P(("zh", "y"), None),
        ),
        out_specs=rows,
        check_vma=False,
    )
```
